32 devices in a mesh: ctx: 16 (over z, y, core), exp: 2 (over x).
Axes of the slice: x: 2, y: 2, z: 4, core: 2. Of those that a mesh axis runs over, the one named last changes fastest.
Arguments:
- queries: bfloat16 [256, 16, 128], P(('exp', 'ctx')), may hold values from -6 to 6
- key_heads: bfloat16 [256, 8, 128], P('ctx', 'exp'), may hold values from -6 to 6
- value_heads: bfloat16 [256, 8, 128], P('ctx', 'exp'), may hold values from -6 to 6
- expert_ids: int32 [256, 16], P(('exp', 'ctx')), may hold values from 0 to 63, all different within a row; in each aligned block of 8 rows (0 to 7, 8 to 15, ...) at most 3 rows name the same one
- gate_logits: float32 [256, 16], P(('exp', 'ctx')), may hold values from -4 to 4
- out_weight: bfloat16 [64, 128, 8192], P('exp', None, 'ctx'), may hold values from -0.5 to 0.5
Outputs:
- mixed_out: bfloat16 [256, 8192], P('exp', 'ctx')
The draws below stay inside these ranges and needn't reach their ends.
Inputs may be any that keep to these rules, and one draw needn't show every extreme that they name: `expert_ids`: each token names 16 different experts; among the 8 tokens of an aligned block no expert is named by more than 3 tokens, a bound that some block reaches.
All inputs are finite; a program needn't handle non-finite values.
Results may differ from the reference program's by a relative error of at most 0.018.
Values may be sent and summed in bfloat16 or wider, within the bound.
A program may use at most 64 MiB of HBM per device.

```python
import math
import jax
import jax.numpy as jnp
import numpy as np
from jax import lax

D = 8192
EXPERTS = 64
KVH = 8
HD = 128
TOP = 16
TOK_DEV = 8
MOST = 3
TOKENS = 256
N_EXP = 2


def draw_queries(key, part):
    drawn = jnp.clip(1.5 * jax.random.normal(jax.random.fold_in(key, 21), (TOKENS, TOP, HD), jnp.float32), -6.0, 6.0)
    return drawn.astype(jnp.bfloat16)


def draw_key_heads(key, part):
    drawn = jnp.clip(jax.random.normal(jax.random.fold_in(key, 22), (TOKENS, KVH, HD), jnp.float32), -6.0, 6.0)
    return drawn.astype(jnp.bfloat16)


def steps_of(key, shape, split, least, high):
    level = 1.0
    for axis_at, blocks in split:
        draws = jax.random.uniform(jax.random.fold_in(jax.random.fold_in(key, 6), axis_at), (blocks,), jnp.float32, least / len(split), high / len(split))
        level = level * jnp.repeat(jnp.exp(draws), shape[axis_at] // blocks).reshape((-1,) + (1,) * (len(shape) - 1 - axis_at))
    return level


def routed_block(stream_key, own, number, rows, amount, top, bound, skew):
    ranking = jax.random.permutation(stream_key, amount)
    heavy_load, usual = shares(amount, rows * top, bound, skew, True), shares(amount, rows * top, bound, skew, False)
    places = jnp.arange(amount)

    def named(tallies, turn):
        used = int((tallies > 0).sum())
        fixed = max(1, used // 4)
        passed = fixed + (places - fixed + turn * (used - fixed)) % max(1, amount - fixed)
        return jnp.zeros((amount,), jnp.int32).at[ranking[jnp.where(places < fixed, places, passed)]].set(jnp.asarray(tallies, jnp.int32))

    tallies = jnp.where(number % 4 == 0, named(heavy_load, number // 4), named(usual, number - number // 4 - 1))
    mixed = jax.random.permutation(jax.random.fold_in(own, 3), amount)
    donor, taker = mixed[0:amount // 2 * 2:2], mixed[1:amount // 2 * 2:2]
    slack = jnp.minimum(tallies[donor] - 1, bound - tallies[taker]) // 2
    slack = jnp.where((donor == ranking[0]) | (taker == ranking[0]) | (tallies[taker] == 0), 0, jnp.maximum(slack, 0))
    passed = jax.random.randint(jax.random.fold_in(own, 4), (amount // 2,), 0, 1 << 20) % (slack + 1)
    tallies = tallies.at[donor].add(-passed).at[taker].add(passed)
    members = jnp.searchsorted(jnp.cumsum(tallies), jnp.arange(rows * top), side="right").astype(jnp.int32)
    listing = members.reshape(top, rows).T
    listing = listing[jax.random.permutation(jax.random.fold_in(own, 1), rows)]
    turn = jax.random.randint(jax.random.fold_in(own, 2), (rows, 1), 0, top)
    return jnp.take_along_axis(listing, (jnp.arange(top)[None, :] + turn) % top, axis=1)


def shares(amount, total, reach, slope, full):
    weights = [(1 << 20) // math.isqrt(standing ** slope) + 1 for standing in range(1, amount + 1)]
    largest = reach if full else min(reach, max(-(-total // amount), total * weights[0] // sum(weights)))
    least = 1 if total - largest >= amount - 1 else 0
    given, surplus = [largest] + [least] * (amount - 1), total - largest - least * (amount - 1)
    while surplus > 0:
        movable = [i for i in range(1, amount) if given[i] < largest] or [i for i in range(1, amount) if given[i] < reach]
        whole, remaining = sum([weights[i] for i in movable]), surplus
        for i in movable:
            extra = min(reach - given[i], max(1, remaining * weights[i] // whole), surplus)
            given[i] = given[i] + extra
            surplus = surplus - extra
    return np.array(given)


def bell_draw(own_key, extent, scale, reach, split=(), kind=jnp.bfloat16):
    values = scale * jax.random.normal(own_key, extent, jnp.float32)
    if split:
        values = values * steps_of(own_key, extent, split, -0.22, 0.18)
    return jnp.clip(values, -reach, reach).astype(kind)


def setup_inputs(seed: int = 0) -> dict:
    streams_of = jax.random.split(jax.random.key(seed), 7)
    queries = draw_queries(jax.random.fold_in(streams_of[6], 71), 0)
    key_heads = draw_key_heads(jax.random.fold_in(streams_of[6], 71), 0)
    value_heads = bell_draw(streams_of[2], (TOKENS, KVH, HD), 1.0, 6.0, ((0, 16), (1, 2)))
    expert_ids_keys = jax.random.split(jax.random.fold_in(streams_of[3], 1), TOKENS // TOK_DEV)
    expert_ids_turns = jax.random.permutation(jax.random.fold_in(streams_of[3], 3), TOKENS // TOK_DEV)
    expert_ids = jax.vmap(lambda own, number: routed_block(jax.random.fold_in(streams_of[3], 2), own, number, TOK_DEV, EXPERTS, TOP, MOST, 2))(expert_ids_keys, expert_ids_turns).reshape((TOKENS, TOP))
    gate_logits = jnp.clip(jax.random.uniform(streams_of[4], (TOKENS, TOP), jnp.float32, -4.0, 4.0) * steps_of(streams_of[4], (TOKENS, TOP), ((0, 32),), -0.4, 0.0), -4.0, 4.0)
    out_weight = bell_draw(streams_of[5], (EXPERTS, HD, D), HD ** -0.5, 0.5, ((0, 2), (2, 16)))
    return dict(queries=queries, key_heads=key_heads, value_heads=value_heads, expert_ids=expert_ids, gate_logits=gate_logits, out_weight=out_weight)


NEG_FLOOR = -1e30


def reference(queries, key_heads, value_heads, expert_ids, gate_logits, out_weight):
    gate_exp = jnp.exp(gate_logits)
    gate_values = (gate_exp / jnp.sum(gate_exp, axis=1, keepdims=True)).astype(jnp.bfloat16)
    group_size = EXPERTS // KVH
    head_of = expert_ids // group_size
    block_tokens = 128
    key_pos = jnp.arange(TOKENS, dtype=jnp.int32)

    def one_head(head_num, collected):
        head_keys = lax.dynamic_index_in_dim(key_heads, head_num, 1, keepdims=False)
        head_values = lax.dynamic_index_in_dim(value_heads, head_num, 1, keepdims=False)

        def one_block(block_num):
            block_queries = lax.dynamic_slice_in_dim(queries, block_num * block_tokens, block_tokens, 0)
            block_queries = block_queries.reshape(block_tokens * TOP, HD)
            query_pos = block_num * block_tokens + jnp.arange(block_tokens * TOP, dtype=jnp.int32) // TOP
            scores = jnp.dot(block_queries, head_keys.T, preferred_element_type=jnp.float32) * (HD ** -0.5)
            visible = key_pos[None, :] <= query_pos[:, None]
            scores = jnp.where(visible, scores, NEG_FLOOR)
            row_max = jnp.max(scores, axis=1, keepdims=True)
            exponents = jnp.where(visible, jnp.exp(scores - row_max), 0.0)
            weighted = jnp.dot(exponents.astype(jnp.bfloat16), head_values, preferred_element_type=jnp.float32)
            normed = weighted / jnp.sum(exponents, axis=1, keepdims=True)
            return normed.reshape(block_tokens, TOP, HD)

        head_out = lax.map(one_block, jnp.arange(TOKENS // block_tokens, dtype=jnp.int32))
        head_out = head_out.reshape(TOKENS, TOP, HD)
        return collected + jnp.where((head_of == head_num)[:, :, None], head_out, 0.0)

    attended = lax.fori_loop(0, KVH, one_head, jnp.zeros((TOKENS, TOP, HD), jnp.float32))
    gated_rows = (gate_values.astype(jnp.float32)[:, :, None] * attended).astype(jnp.bfloat16)
    per_device = EXPERTS // N_EXP

    def one_group(group_num, accumulated):
        def one_expert(local_num, partial_value):
            expert_num = group_num * per_device + local_num
            chosen = jnp.sum(jnp.where((expert_ids == expert_num)[:, :, None], gated_rows.astype(jnp.float32), 0.0), axis=1)
            chosen = chosen.astype(jnp.bfloat16)
            weight_now = lax.dynamic_index_in_dim(out_weight, expert_num, 0, keepdims=False)
            return partial_value + jnp.dot(chosen, weight_now, preferred_element_type=jnp.float32)

        partial_value = lax.fori_loop(0, per_device, one_expert, jnp.zeros((TOKENS, D), jnp.float32))
        rounded = lax.optimization_barrier(partial_value.astype(jnp.bfloat16))
        return accumulated + rounded.astype(jnp.float32)

    accumulated = lax.fori_loop(0, N_EXP, one_group, jnp.zeros((TOKENS, D), jnp.float32))
    return accumulated.astype(jnp.bfloat16)
```

```python
import functools

import jax
import jax.numpy as jnp
from jax import lax
from jax.experimental import pallas as pl
from jax.experimental.pallas import tpu as pltpu
from jax.sharding import PartitionSpec as P

EXPERTS = 64
MOST = 3
LANES = 128
META_ROWS = 16
F32 = jnp.float32
BF16 = jnp.bfloat16
MESH = pl.DeviceIdType.MESH


def iota(shape, dim):
    return lax.broadcasted_iota(jnp.int32, shape, dim)


def flood(buf, send, recv, coords, n, use):
    slow, mid, last, slows = coords
    me = (slow * 2 + mid) * 2 + last
    mid_peer = (slow * 2 + (1 - mid)) * 2 + last
    last_peer = (slow * 2 + mid) * 2 + (1 - last)

    def copy(kind, slot, src, to):
        return pltpu.make_async_remote_copy(
            src_ref=buf.at[src],
            dst_ref=buf.at[src],
            send_sem=send.at[kind, slot],
            recv_sem=recv.at[src],
            device_id={"ctx": to},
            device_id_type=MESH,
        )

    def slow_peer(k):
        return (lax.rem(slow + k, slows) * 2 + mid) * 2 + last

    for k in range(1, slows):
        copy(0, k, me, slow_peer(k)).start()
    copy(1, me, me, mid_peer).start()
    copy(2, me, me, last_peer).start()
    use(me)

    @pl.loop(1, slows)
    def _(k):
        src = slow_peer(k)
        copy(0, k, src, mid_peer).wait_recv()
        copy(1, src, src, mid_peer).start()
        copy(2, src, src, last_peer).start()
        use(src)

    @pl.loop(0, slows)
    def _(k):
        src = (lax.rem(slow + k, slows) * 2 + (1 - mid)) * 2 + last
        copy(1, src, src, mid_peer).wait_recv()
        copy(2, src, src, last_peer).start()
        use(src)

    @pl.loop(0, slows * 2)
    def _(k):
        src = (lax.rem(slow + k // 2, slows) * 2 + lax.rem(mid + lax.rem(k, 2), 2)) * 2 + (1 - last)
        copy(2, src, src, last_peer).wait_recv()
        use(src)

    for k in range(1, slows):
        copy(0, k, me, slow_peer(k)).wait_send()

    @pl.loop(0, slows)
    def _(k):
        own = (k * 2 + mid) * 2 + last
        other = (k * 2 + (1 - mid)) * 2 + last
        copy(1, own, own, mid_peer).wait_send()
        copy(2, own, own, last_peer).wait_send()
        copy(2, other, other, last_peer).wait_send()


def kernel(n, E, top, q_ref, kv_ref, ids_ref, gate_ref, w_hbm, out_ref,
           q_all, meta_all, kv_all, g_all, dense, w_all, part_in, part_out, acc,
           kv_send, kv_recv, g_send, g_recv, q_send, q_recv, m_send, m_recv, p_send, p_recv, w_sem):
    ctx = lax.axis_index("ctx")
    me = lax.axis_index("exp")
    slows = n // 4
    slow, mid, last = ctx // 4, lax.rem(ctx // 2, 2), lax.rem(ctx, 2)
    coords = (slow, mid, last, slows)
    rows, hd = q_ref.shape
    tok_dev = rows // top
    span = kv_ref.shape[0]
    heads = kv_ref.shape[1] // (2 * hd)
    per_dev = EXPERTS // E
    group = per_dev // heads
    slots = g_all.shape[2] - META_ROWS
    cols = w_all.shape[1]
    keys = n * span

    w_copy = pltpu.make_async_copy(w_hbm, w_all, w_sem)
    w_copy.start()

    barrier = pltpu.get_barrier_semaphore()
    for k in range(1, slows):
        pl.semaphore_signal(barrier, inc=1, device_id={"ctx": (lax.rem(slow + k, slows) * 2 + mid) * 2 + last}, device_id_type=MESH)
    pl.semaphore_signal(barrier, inc=1, device_id={"ctx": (slow * 2 + 1 - mid) * 2 + last}, device_id_type=MESH)
    pl.semaphore_signal(barrier, inc=1, device_id={"ctx": (slow * 2 + mid) * 2 + 1 - last}, device_id_type=MESH)
    for k in range(1, E):
        pl.semaphore_signal(barrier, inc=1, device_id={"exp": lax.rem(me + k, E)}, device_id_type=MESH)

    diag = iota((rows, rows), 0) == iota((rows, rows), 1)

    def to_lanes(values):
        spread = jnp.concatenate(
            [jnp.broadcast_to(values[t : t + 1, :], (top, top)) for t in range(tok_dev)], 0
        )
        mine = lax.rem(iota((rows, top), 0), top) == iota((rows, top), 1)
        column = jnp.sum(jnp.where(mine, spread, 0.0), axis=1, keepdims=True)
        return jnp.sum(jnp.where(diag, column, 0.0), axis=0, keepdims=True)

    def to_column(lane_row):
        return jnp.sum(jnp.where(diag, lane_row, 0.0), axis=1, keepdims=True)

    gate_exp = jnp.exp(gate_ref[...])
    gates = (gate_exp / jnp.sum(gate_exp, axis=1, keepdims=True)).astype(BF16).astype(F32)
    meta_all[me] = jnp.concatenate(
        [
            jnp.broadcast_to(to_lanes(ids_ref[...].astype(F32)), (4, rows)),
            jnp.broadcast_to(to_lanes(gates), (4, rows)),
        ],
        0,
    )
    q_all[me] = q_ref[...]
    kv_all[ctx] = kv_ref[...]

    pl.semaphore_wait(barrier, slows - 1 + 2 + E - 1)

    def exchange(buf, send, recv, k, src):
        return pltpu.make_async_remote_copy(
            src_ref=buf.at[src],
            dst_ref=buf.at[src],
            send_sem=send.at[k],
            recv_sem=recv.at[src],
            device_id={"exp": lax.rem(me + k, E)},
            device_id_type=MESH,
        )

    for k in range(1, E):
        exchange(q_all, q_send, q_recv, k, me).start()
        exchange(meta_all, m_send, m_recv, k, me).start()
    flood(kv_all, kv_send, kv_recv, coords, n, lambda src: None)
    for k in range(1, E):
        src = lax.rem(me + k, E)
        exchange(q_all, q_send, q_recv, k, src).wait_recv()
        exchange(meta_all, m_send, m_recv, k, src).wait_recv()

    @pl.loop(0, E)
    def _(b):
        meta = meta_all[b]
        local = meta[0:1, :] - (me * per_dev).astype(F32)
        inside_row = (local >= 0.0) & (local < per_dev)
        local_col = to_column(local)
        gate_col = to_column(meta[4:5, :])
        inside_col = (local_col >= 0.0) & (local_col < per_dev)
        q = q_all[b]
        scores = jnp.zeros((rows, keys), F32)
        of_head = [
            (local_col >= h * group) & (local_col < (h + 1) * group) for h in range(heads)
        ]
        for h in range(heads):
            k_h = kv_all[:, :, h * hd : (h + 1) * hd].reshape(keys, hd)
            s_h = lax.dot_general(q, k_h, (((1,), (1,)), ((), ())), preferred_element_type=F32)
            scores = jnp.where(of_head[h], s_h, scores)
        scores = scores * hd ** (-0.5)
        first = (b * n + ctx) * tok_dev
        visible = iota((rows, keys), 1) <= first + iota((rows, keys), 0) // top
        scores = jnp.where(visible, scores, -1e30)
        peak = jnp.max(scores, axis=1, keepdims=True)
        weights = jnp.where(visible, jnp.exp(scores - peak), 0.0)
        total = jnp.sum(weights, axis=1, keepdims=True)
        mixed = jnp.zeros((rows, hd), F32)
        for h in range(heads):
            v_h = kv_all[:, :, (heads + h) * hd : (heads + h + 1) * hd].reshape(keys, hd)
            mixed += jnp.dot(
                jnp.where(of_head[h], weights, 0.0).astype(BF16), v_h, preferred_element_type=F32
            )
        gated = (gate_col * (mixed / total)).astype(BF16)
        before = (iota((rows, rows), 0) < iota((rows, rows), 1)) & inside_col
        rank_row = jnp.sum(jnp.where(before, 1.0, 0.0), axis=0, keepdims=True)
        slot_row = jnp.where(inside_row, rank_row, -1.0)
        slot_col = to_column(slot_row)
        pick = (iota((slots, rows), 0).astype(F32) == slot_row).astype(F32).astype(BF16)
        packed = jnp.dot(pick, gated, preferred_element_type=F32).astype(BF16)
        place = local_col * tok_dev + (iota((rows, 1), 0) // top).astype(F32)
        placed = slot_col == iota((rows, LANES), 1).astype(F32)
        target = jnp.sum(jnp.where(placed, place + 1.0, 0.0), axis=0, keepdims=True) - 1.0
        g_all[ctx, b, 0:slots, :] = packed
        g_all[ctx, b, slots : slots + META_ROWS, :] = jnp.broadcast_to(
            target, (META_ROWS, LANES)
        ).astype(BF16)

    def expand(src):
        for b in range(E):
            shard = g_all[src, b]
            target = shard[slots:, :].astype(F32)[0:1, : slots + META_ROWS]
            where = (
                iota((per_dev * tok_dev, slots + META_ROWS), 0).astype(F32) == target
            ).astype(F32).astype(BF16)
            spread = jnp.dot(where, shard, preferred_element_type=F32)
            at = pl.ds(pl.multiple_of((b * n + src) * tok_dev, tok_dev), tok_dev)
            for x in range(per_dev):
                dense[at, x * hd : (x + 1) * hd] = spread[x * tok_dev : (x + 1) * tok_dev, :]

    flood(g_all, g_send, g_recv, coords, n, expand)
    w_copy.wait()

    half = n * tok_dev
    depth = per_dev * hd
    chunk = min(512, depth)

    def project(b):
        acc[...] = jnp.zeros_like(acc)
        base = pl.multiple_of(b * half, half)

        @pl.loop(0, depth // chunk)
        def _(j):
            at = pl.ds(pl.multiple_of(j * chunk, chunk), chunk)
            acc[...] += jnp.dot(
                dense[pl.ds(base, half), at].astype(BF16), w_all[at, :], preferred_element_type=F32
            )

    def send_part(k):
        return pltpu.make_async_remote_copy(
            src_ref=part_out.at[k],
            dst_ref=part_in.at[E - k],
            send_sem=p_send.at[k],
            recv_sem=p_recv.at[E - k],
            device_id={"exp": lax.rem(me + k, E)},
            device_id_type=MESH,
        )

    for k in range(1, E):
        project(lax.rem(me + k, E))
        part_out[k] = acc[...].astype(BF16)
        send_part(k).start()
    project(me)
    total = acc[...].astype(BF16).astype(F32)
    for k in range(1, E):
        send_part(E - k).wait_recv()
        total += part_in[k].astype(F32)
    out_ref[...] = total.astype(BF16)
    for k in range(1, E):
        send_part(k).wait_send()
        exchange(q_all, q_send, q_recv, k, me).wait_send()
        exchange(meta_all, m_send, m_recv, k, me).wait_send()


def body(queries, key_heads, value_heads, expert_ids, gate_logits, out_weight):
    n = lax.axis_size("ctx")
    E = lax.axis_size("exp")
    tok_dev, top, hd = queries.shape
    rows = tok_dev * top
    span, heads, _ = key_heads.shape
    per_dev, _, cols = out_weight.shape
    slots = -(-per_dev * MOST // 16) * 16
    kv = jnp.concatenate(
        [key_heads.reshape(span, heads * hd), value_heads.reshape(span, heads * hd)], axis=1
    )
    vmem = pl.BlockSpec(memory_space=pltpu.VMEM)
    dma = pltpu.SemaphoreType.DMA
    return pl.pallas_call(
        functools.partial(kernel, n, E, top),
        out_shape=jax.ShapeDtypeStruct((n * tok_dev, cols), BF16),
        in_specs=[vmem] * 4 + [pl.BlockSpec(memory_space=pl.ANY)],
        out_specs=vmem,
        scratch_shapes=[
            pltpu.VMEM((E, rows, hd), BF16),
            pltpu.VMEM((E, 8, rows), F32),
            pltpu.VMEM((n, span, 2 * heads * hd), BF16),
            pltpu.VMEM((n, E, slots + META_ROWS, hd), BF16),
            pltpu.VMEM((E * n * tok_dev, per_dev * hd), F32),
            pltpu.VMEM((per_dev * hd, cols), BF16),
            pltpu.VMEM((E, n * tok_dev, cols), BF16),
            pltpu.VMEM((E, n * tok_dev, cols), BF16),
            pltpu.VMEM((n * tok_dev, cols), F32),
            dma((3, n)), dma((n,)), dma((3, n)), dma((n,)),
            dma((E,)), dma((E,)), dma((E,)), dma((E,)), dma((E,)), dma((E,)),
            dma,
        ],
        compiler_params=pltpu.CompilerParams(
            collective_id=0, has_side_effects=True, vmem_limit_bytes=50 * 2**20
        ),
    )(queries.reshape(rows, hd), kv, expert_ids, gate_logits, out_weight.reshape(per_dev * hd, cols))


def solution(mesh):
    in_specs = (
        P(("exp", "ctx"), None, None),
        P("ctx", "exp", None),
        P("ctx", "exp", None),
        P(("exp", "ctx"), None),
        P(("exp", "ctx"), None),
        P("exp", None, "ctx"),
    )
    out_specs = P("exp", "ctx")
    return jax.shard_map(body, mesh=mesh, in_specs=in_specs, out_specs=out_specs, check_vma=False)
```

```python
import functools

import jax
import jax.numpy as jnp
from jax import lax
from jax.experimental import pallas as pl
from jax.experimental.pallas import tpu as pltpu
from jax.sharding import PartitionSpec as P

EXPERTS = 64
MOST = 3
LANES = 128
META_ROWS = 16
F32 = jnp.float32
BF16 = jnp.bfloat16
MESH = pl.DeviceIdType.MESH


def iota(shape, dim):
    return lax.broadcasted_iota(jnp.int32, shape, dim)


class Flood:
    def __init__(self, buf, send, recv, ctx, n):
        self.buf, self.send, self.recv = buf, send, recv
        self.units, self.slows, self.me = buf.shape[1], n // 4, ctx
        self.slow, self.mid, self.last = ctx // 4, lax.rem(ctx // 2, 2), lax.rem(ctx, 2)
        self.mid_peer = (self.slow * 2 + (1 - self.mid)) * 2 + self.last
        self.last_peer = (self.slow * 2 + self.mid) * 2 + (1 - self.last)

    def copy(self, kind, slot, src, u, to):
        return pltpu.make_async_remote_copy(
            src_ref=self.buf.at[src, u],
            dst_ref=self.buf.at[src, u],
            send_sem=self.send.at[kind, slot, u],
            recv_sem=self.recv.at[src, u],
            device_id={"ctx": to},
            device_id_type=MESH,
        )

    def slow_peer(self, k):
        return (lax.rem(self.slow + k, self.slows) * 2 + self.mid) * 2 + self.last

    def over_mid(self, src, u):
        return self.copy(1, src, src, u, self.mid_peer)

    def over_last(self, src, u):
        return self.copy(2, src, src, u, self.last_peer)

    def begin(self, u):
        for k in range(1, self.slows):
            self.copy(0, k, self.me, u, self.slow_peer(k)).start()
        self.over_mid(self.me, u).start()
        self.over_last(self.me, u).start()

    def from_slow(self, u, use):
        @pl.loop(1, self.slows)
        def _(k):
            src = self.slow_peer(k)
            self.over_mid(src, u).wait_recv()
            self.over_mid(src, u).start()
            self.over_last(src, u).start()
            use(src, u)

    def from_mid(self, u, use):
        @pl.loop(0, self.slows)
        def _(k):
            src = (lax.rem(self.slow + k, self.slows) * 2 + (1 - self.mid)) * 2 + self.last
            self.over_mid(src, u).wait_recv()
            self.over_last(src, u).start()
            use(src, u)

    def from_last(self, u, use):
        @pl.loop(0, self.slows * 2)
        def _(k):
            m = lax.rem(self.mid + k // self.slows, 2)
            src = (lax.rem(self.slow + k, self.slows) * 2 + m) * 2 + (1 - self.last)
            self.over_last(src, u).wait_recv()
            use(src, u)

    def end(self):
        @pl.loop(0, self.units)
        def _(u):
            for k in range(1, self.slows):
                self.copy(0, k, self.me, u, self.slow_peer(k)).wait_send()

            @pl.loop(0, self.slows)
            def _(k):
                own = (k * 2 + self.mid) * 2 + self.last
                other = (k * 2 + (1 - self.mid)) * 2 + self.last
                self.over_mid(own, u).wait_send()
                self.over_last(own, u).wait_send()
                self.over_last(other, u).wait_send()


def kernel(n, E, top, q_hbm, k_hbm, v_hbm, ids_hbm, gate_hbm, w_hbm, out_ref,
           k_ref, v_ref, ids_ref, gate_ref, q_all, meta_all, kv_all, g_all, dense, w_all, part_in, part_out, acc,
           kv_send, kv_recv, g_send, g_recv, q_send, q_recv, m_send, m_recv, p_send, p_recv, w_sem, in_sem):
    ctx = lax.axis_index("ctx")
    me = lax.axis_index("exp")
    slows = n // 4
    slow, mid, last = ctx // 4, lax.rem(ctx // 2, 2), lax.rem(ctx, 2)
    rows, hd = q_hbm.shape
    tok_dev = rows // top
    span, heads = k_hbm.shape[0], k_hbm.shape[1]
    per_dev = EXPERTS // E
    group = per_dev // heads
    slots = g_all.shape[2] - META_ROWS
    keys = n * span

    inputs = [
        pltpu.make_async_copy(a, b, in_sem.at[k])
        for k, (a, b) in enumerate(
            [(k_hbm, k_ref), (v_hbm, v_ref), (ids_hbm, ids_ref), (gate_hbm, gate_ref), (q_hbm, q_all.at[me])]
        )
    ]
    for copy in inputs:
        copy.start()
    w_copy = pltpu.make_async_copy(w_hbm, w_all, w_sem)

    barrier = pltpu.get_barrier_semaphore()
    for k in range(1, slows):
        pl.semaphore_signal(barrier, inc=1, device_id={"ctx": (lax.rem(slow + k, slows) * 2 + mid) * 2 + last}, device_id_type=MESH)
    pl.semaphore_signal(barrier, inc=1, device_id={"ctx": (slow * 2 + 1 - mid) * 2 + last}, device_id_type=MESH)
    pl.semaphore_signal(barrier, inc=1, device_id={"ctx": (slow * 2 + mid) * 2 + 1 - last}, device_id_type=MESH)
    for k in range(1, E):
        pl.semaphore_signal(barrier, inc=1, device_id={"exp": lax.rem(me + k, E)}, device_id_type=MESH)

    for copy in inputs:
        copy.wait()
    diag = iota((rows, rows), 0) == iota((rows, rows), 1)

    def to_lanes(values):
        spread = jnp.concatenate(
            [jnp.broadcast_to(values[t : t + 1, :], (top, top)) for t in range(tok_dev)], 0
        )
        mine = lax.rem(iota((rows, top), 0), top) == iota((rows, top), 1)
        column = jnp.sum(jnp.where(mine, spread, 0.0), axis=1, keepdims=True)
        return jnp.sum(jnp.where(diag, column, 0.0), axis=0, keepdims=True)

    def to_column(lane_row):
        return jnp.sum(jnp.where(diag, lane_row, 0.0), axis=1, keepdims=True)

    gate_exp = jnp.exp(gate_ref[...])
    gates = (gate_exp / jnp.sum(gate_exp, axis=1, keepdims=True)).astype(BF16).astype(F32)
    meta_all[me] = jnp.concatenate(
        [
            jnp.broadcast_to(to_lanes(ids_ref[...].astype(F32)), (4, rows)),
            jnp.broadcast_to(to_lanes(gates), (4, rows)),
        ],
        0,
    )
    for h in range(heads):
        kv_all[ctx, 0, :, h * hd : (h + 1) * hd] = k_ref[...].astype(F32)[:, h, :].astype(BF16)
        kv_all[ctx, 0, :, (heads + h) * hd : (heads + h + 1) * hd] = v_ref[...].astype(F32)[:, h, :].astype(BF16)

    pl.semaphore_wait(barrier, slows - 1 + 2 + E - 1)

    def exchange(buf, send, recv, k, src):
        return pltpu.make_async_remote_copy(
            src_ref=buf.at[src],
            dst_ref=buf.at[src],
            send_sem=send.at[k],
            recv_sem=recv.at[src],
            device_id={"exp": lax.rem(me + k, E)},
            device_id_type=MESH,
        )

    kv_flood = Flood(kv_all, kv_send, kv_recv, ctx, n)
    g_flood = Flood(g_all, g_send, g_recv, ctx, n)
    kv_flood.begin(0)
    for k in range(1, E):
        exchange(q_all, q_send, q_recv, k, me).start()
        exchange(meta_all, m_send, m_recv, k, me).start()
    w_copy.start()
    for step in (kv_flood.from_slow, kv_flood.from_mid, kv_flood.from_last):
        step(0, lambda src, u: None)
    for k in range(1, E):
        src = lax.rem(me + k, E)
        exchange(q_all, q_send, q_recv, k, src).wait_recv()
        exchange(meta_all, m_send, m_recv, k, src).wait_recv()

    @pl.loop(0, E)
    def _(i):
        b = lax.rem(me + 1 + i, E)
        meta = meta_all[b]
        local = meta[0:1, :] - (me * per_dev).astype(F32)
        inside_row = (local >= 0.0) & (local < per_dev)
        local_col = to_column(local)
        gate_col = to_column(meta[4:5, :])
        inside_col = (local_col >= 0.0) & (local_col < per_dev)
        q = q_all[b]
        scores = jnp.zeros((rows, keys), F32)
        of_head = [
            (local_col >= h * group) & (local_col < (h + 1) * group) for h in range(heads)
        ]
        for h in range(heads):
            k_h = kv_all[:, 0, :, h * hd : (h + 1) * hd].reshape(keys, hd)
            s_h = lax.dot_general(q, k_h, (((1,), (1,)), ((), ())), preferred_element_type=F32)
            scores = jnp.where(of_head[h], s_h, scores)
        scores = scores * hd ** (-0.5)
        first = (b * n + ctx) * tok_dev
        visible = iota((rows, keys), 1) <= first + iota((rows, keys), 0) // top
        scores = jnp.where(visible, scores, -1e30)
        peak = jnp.max(scores, axis=1, keepdims=True)
        weights = jnp.where(visible, jnp.exp(scores - peak), 0.0)
        total = jnp.sum(weights, axis=1, keepdims=True)
        mixed = jnp.zeros((rows, hd), F32)
        for h in range(heads):
            v_h = kv_all[:, 0, :, (heads + h) * hd : (heads + h + 1) * hd].reshape(keys, hd)
            mixed += jnp.dot(
                jnp.where(of_head[h], weights, 0.0).astype(BF16), v_h, preferred_element_type=F32
            )
        gated = (gate_col * (mixed / total)).astype(BF16)
        before = (iota((rows, rows), 0) < iota((rows, rows), 1)) & inside_col
        rank_row = jnp.sum(jnp.where(before, 1.0, 0.0), axis=0, keepdims=True)
        slot_row = jnp.where(inside_row, rank_row, -1.0)
        slot_col = to_column(slot_row)
        pick = (iota((slots, rows), 0).astype(F32) == slot_row).astype(F32).astype(BF16)
        packed = jnp.dot(pick, gated, preferred_element_type=F32).astype(BF16)
        place = local_col * tok_dev + (iota((rows, 1), 0) // top).astype(F32)
        placed = slot_col == iota((rows, LANES), 1).astype(F32)
        target = jnp.sum(jnp.where(placed, place + 1.0, 0.0), axis=0, keepdims=True) - 1.0
        g_all[ctx, b, 0:slots, :] = packed
        g_all[ctx, b, slots : slots + META_ROWS, :] = jnp.broadcast_to(
            target, (META_ROWS, LANES)
        ).astype(BF16)
        g_flood.begin(b)

    def expand(src, b):
        shard = g_all[src, b]
        target = shard[slots:, :].astype(F32)[0:1, : slots + META_ROWS]
        where = (
            iota((per_dev * tok_dev, slots + META_ROWS), 0).astype(F32) == target
        ).astype(F32).astype(BF16)
        spread = jnp.dot(where, shard, preferred_element_type=F32)
        at = pl.ds(pl.multiple_of((b * n + src) * tok_dev, tok_dev), tok_dev)
        for x in range(per_dev):
            dense[at, x * hd : (x + 1) * hd] = spread[x * tok_dev : (x + 1) * tok_dev, :]

    half = n * tok_dev
    depth = per_dev * hd
    chunk = min(512, depth)
    parts, width = part_in.shape[1], part_in.shape[3]

    def project(b, p):
        acc[...] = jnp.zeros_like(acc)
        base = pl.multiple_of(b * half, half)

        @pl.loop(0, depth // chunk)
        def _(j):
            at = pl.ds(pl.multiple_of(j * chunk, chunk), chunk)
            acc[...] += jnp.dot(
                dense[pl.ds(base, half), at].astype(BF16),
                w_all[at, p * width : (p + 1) * width],
                preferred_element_type=F32,
            )
        return acc[...].astype(BF16)

    def send_part(k, p):
        return pltpu.make_async_remote_copy(
            src_ref=part_out.at[k, p],
            dst_ref=part_in.at[E - k, p],
            send_sem=p_send.at[k, p],
            recv_sem=p_recv.at[E - k, p],
            device_id={"exp": lax.rem(me + k, E)},
            device_id_type=MESH,
        )

    w_copy.wait()
    halves = [lax.rem(me + 1 + i, E) for i in range(E)]

    def finish(i):
        k = (i + 1) % E
        for p in range(parts):
            part_out[k, p] = project(halves[i], p)
            if k:
                send_part(k, p).start()

    for i in range(E):
        g_flood.from_slow(halves[i], expand)
        if i:
            g_flood.from_last(halves[i - 1], expand)
            expand(ctx, halves[i - 1])
            finish(i - 1)
        g_flood.from_mid(halves[i], expand)
    g_flood.from_last(me, expand)
    expand(ctx, me)
    finish(E - 1)
    kv_flood.end()
    g_flood.end()
    for k in range(1, E):
        exchange(q_all, q_send, q_recv, k, me).wait_send()
        exchange(meta_all, m_send, m_recv, k, me).wait_send()
    for p in range(parts):
        total = part_out[0, p].astype(F32)
        for k in range(1, E):
            send_part(E - k, p).wait_recv()
            total += part_in[k, p].astype(F32)
        out_ref[:, p * width : (p + 1) * width] = total.astype(BF16)
    for k in range(1, E):
        for p in range(parts):
            send_part(k, p).wait_send()


def body(queries, key_heads, value_heads, expert_ids, gate_logits, out_weight):
    n = lax.axis_size("ctx")
    E = lax.axis_size("exp")
    tok_dev, top, hd = queries.shape
    rows = tok_dev * top
    span, heads, _ = key_heads.shape
    per_dev, _, cols = out_weight.shape
    slots = -(-per_dev * MOST // 16) * 16
    parts = max(1, cols // 256)
    vmem = pl.BlockSpec(memory_space=pltpu.VMEM)
    dma = pltpu.SemaphoreType.DMA
    return pl.pallas_call(
        functools.partial(kernel, n, E, top),
        out_shape=jax.ShapeDtypeStruct((n * tok_dev, cols), BF16),
        in_specs=[pl.BlockSpec(memory_space=pltpu.HBM)] * 6,
        out_specs=vmem,
        scratch_shapes=[
            pltpu.VMEM((span, heads, hd), BF16),
            pltpu.VMEM((span, heads, hd), BF16),
            pltpu.VMEM((tok_dev, top), jnp.int32),
            pltpu.VMEM((tok_dev, top), F32),
            pltpu.VMEM((E, rows, hd), BF16),
            pltpu.VMEM((E, 8, rows), F32),
            pltpu.VMEM((n, 1, span, 2 * heads * hd), BF16),
            pltpu.VMEM((n, E, slots + META_ROWS, hd), BF16),
            pltpu.VMEM((E * n * tok_dev, per_dev * hd), F32),
            pltpu.VMEM((per_dev * hd, cols), BF16),
            pltpu.VMEM((E, parts, n * tok_dev, cols // parts), BF16),
            pltpu.VMEM((E, parts, n * tok_dev, cols // parts), BF16),
            pltpu.VMEM((n * tok_dev, cols // parts), F32),
            dma((3, n, 1)), dma((n, 1)), dma((3, n, E)), dma((n, E)),
            dma((E,)), dma((E,)), dma((E,)), dma((E,)), dma((E, parts)), dma((E, parts)),
            dma, dma((5,)),
        ],
        compiler_params=pltpu.CompilerParams(
            collective_id=0, has_side_effects=True, vmem_limit_bytes=50 * 2**20
        ),
    )(queries.reshape(rows, hd), key_heads, value_heads, expert_ids, gate_logits, out_weight.reshape(per_dev * hd, cols))


def solution(mesh):
    in_specs = (
        P(("exp", "ctx"), None, None),
        P("ctx", "exp", None),
        P("ctx", "exp", None),
        P(("exp", "ctx"), None),
        P(("exp", "ctx"), None),
        P("exp", None, "ctx"),
    )
    out_specs = P("exp", "ctx")
    return jax.shard_map(body, mesh=mesh, in_specs=in_specs, out_specs=out_specs, check_vma=False)
```

```python
import functools

import jax
import jax.numpy as jnp
from jax import lax
from jax.experimental import pallas as pl
from jax.experimental.pallas import tpu as pltpu
from jax.sharding import PartitionSpec as P

EXPERTS = 64
MOST = 3
LANES = 128
META_ROWS = 16
F32 = jnp.float32
BF16 = jnp.bfloat16
MESH = pl.DeviceIdType.MESH


def iota(shape, dim):
    return lax.broadcasted_iota(jnp.int32, shape, dim)


class Flood:
    def __init__(self, buf, send, recv, ctx, n):
        self.buf, self.send, self.recv = buf, send, recv
        self.units, self.slows, self.me = buf.shape[1], n // 4, ctx
        self.slow, self.mid, self.last = ctx // 4, lax.rem(ctx // 2, 2), lax.rem(ctx, 2)
        self.mid_peer = (self.slow * 2 + (1 - self.mid)) * 2 + self.last
        self.last_peer = (self.slow * 2 + self.mid) * 2 + (1 - self.last)

    def copy(self, kind, slot, src, u, to):
        return pltpu.make_async_remote_copy(
            src_ref=self.buf.at[src, u],
            dst_ref=self.buf.at[src, u],
            send_sem=self.send.at[kind, slot, u],
            recv_sem=self.recv.at[src, u],
            device_id={"ctx": to},
            device_id_type=MESH,
        )

    def slow_peer(self, k):
        return (lax.rem(self.slow + k, self.slows) * 2 + self.mid) * 2 + self.last

    def over_mid(self, src, u):
        return self.copy(1, src, src, u, self.mid_peer)

    def over_last(self, src, u):
        return self.copy(2, src, src, u, self.last_peer)

    def begin(self, u):
        for k in range(1, self.slows):
            self.copy(0, k, self.me, u, self.slow_peer(k)).start()
        self.over_mid(self.me, u).start()
        self.over_last(self.me, u).start()

    def from_slow(self, u, use):
        @pl.loop(1, self.slows)
        def _(k):
            src = self.slow_peer(k)
            self.over_mid(src, u).wait_recv()
            self.over_mid(src, u).start()
            self.over_last(src, u).start()
            use(src, u)

    def from_mid(self, u, use):
        @pl.loop(0, self.slows)
        def _(k):
            src = (lax.rem(self.slow + k, self.slows) * 2 + (1 - self.mid)) * 2 + self.last
            self.over_mid(src, u).wait_recv()
            self.over_last(src, u).start()
            use(src, u)

    def from_last(self, u, use):
        @pl.loop(0, self.slows * 2)
        def _(k):
            m = lax.rem(self.mid + k // self.slows, 2)
            src = (lax.rem(self.slow + k, self.slows) * 2 + m) * 2 + (1 - self.last)
            self.over_last(src, u).wait_recv()
            use(src, u)

    def end(self):
        @pl.loop(0, self.units)
        def _(u):
            for k in range(1, self.slows):
                self.copy(0, k, self.me, u, self.slow_peer(k)).wait_send()

            @pl.loop(0, self.slows)
            def _(k):
                own = (k * 2 + self.mid) * 2 + self.last
                other = (k * 2 + (1 - self.mid)) * 2 + self.last
                self.over_mid(own, u).wait_send()
                self.over_last(own, u).wait_send()
                self.over_last(other, u).wait_send()


def kernel(n, E, top, q_hbm, k_hbm, v_hbm, ids_hbm, gate_hbm, w_hbm, out_ref,
           k_ref, v_ref, ids_ref, gate_ref, q_all, meta_all, kv_all, g_all, dense, w_all, part_in, part_out, acc,
           kv_send, kv_recv, g_send, g_recv, q_send, q_recv, m_send, m_recv, p_send, p_recv, w_sem, in_sem):
    ctx = lax.axis_index("ctx")
    me = lax.axis_index("exp")
    slows = n // 4
    slow, mid, last = ctx // 4, lax.rem(ctx // 2, 2), lax.rem(ctx, 2)
    rows, hd = q_hbm.shape
    tok_dev = rows // top
    span, heads = k_hbm.shape[0], k_hbm.shape[1]
    per_dev = EXPERTS // E
    group = per_dev // heads
    slots = g_all.shape[2] - META_ROWS
    keys = n * span

    inputs = [
        pltpu.make_async_copy(a, b, in_sem.at[k])
        for k, (a, b) in enumerate(
            [(k_hbm, k_ref), (v_hbm, v_ref), (ids_hbm, ids_ref), (gate_hbm, gate_ref), (q_hbm, q_all.at[me])]
        )
    ]
    for copy in inputs:
        copy.start()
    w_copy = pltpu.make_async_copy(w_hbm, w_all, w_sem)

    barrier = pltpu.get_barrier_semaphore()
    for k in range(1, slows):
        pl.semaphore_signal(barrier, inc=1, device_id={"ctx": (lax.rem(slow + k, slows) * 2 + mid) * 2 + last}, device_id_type=MESH)
    pl.semaphore_signal(barrier, inc=1, device_id={"ctx": (slow * 2 + 1 - mid) * 2 + last}, device_id_type=MESH)
    pl.semaphore_signal(barrier, inc=1, device_id={"ctx": (slow * 2 + mid) * 2 + 1 - last}, device_id_type=MESH)
    for k in range(1, E):
        pl.semaphore_signal(barrier, inc=1, device_id={"exp": lax.rem(me + k, E)}, device_id_type=MESH)

    for copy in inputs:
        copy.wait()
    diag = iota((rows, rows), 0) == iota((rows, rows), 1)

    def to_lanes(values):
        spread = jnp.concatenate(
            [jnp.broadcast_to(values[t : t + 1, :], (top, top)) for t in range(tok_dev)], 0
        )
        mine = lax.rem(iota((rows, top), 0), top) == iota((rows, top), 1)
        column = jnp.sum(jnp.where(mine, spread, 0.0), axis=1, keepdims=True)
        return jnp.sum(jnp.where(diag, column, 0.0), axis=0, keepdims=True)

    def to_column(lane_row):
        return jnp.sum(jnp.where(diag, lane_row, 0.0), axis=1, keepdims=True)

    gate_exp = jnp.exp(gate_ref[...])
    gates = (gate_exp / jnp.sum(gate_exp, axis=1, keepdims=True)).astype(BF16).astype(F32)
    meta_all[me] = jnp.concatenate(
        [
            jnp.broadcast_to(to_lanes(ids_ref[...].astype(F32)), (4, rows)),
            jnp.broadcast_to(to_lanes(gates), (4, rows)),
        ],
        0,
    )
    for h in range(heads):
        kv_all[ctx, 0, :, h * hd : (h + 1) * hd] = k_ref[...].astype(F32)[:, h, :].astype(BF16)
        kv_all[ctx, 0, :, (heads + h) * hd : (heads + h + 1) * hd] = v_ref[...].astype(F32)[:, h, :].astype(BF16)

    pl.semaphore_wait(barrier, slows - 1 + 2 + E - 1)

    def exchange(buf, send, recv, k, src):
        return pltpu.make_async_remote_copy(
            src_ref=buf.at[src],
            dst_ref=buf.at[src],
            send_sem=send.at[k],
            recv_sem=recv.at[src],
            device_id={"exp": lax.rem(me + k, E)},
            device_id_type=MESH,
        )

    kv_flood = Flood(kv_all, kv_send, kv_recv, ctx, n)
    g_flood = Flood(g_all, g_send, g_recv, ctx, n)
    kv_flood.begin(0)
    for k in range(1, E):
        exchange(q_all, q_send, q_recv, k, me).start()
        exchange(meta_all, m_send, m_recv, k, me).start()
    w_copy.start()
    for step in (kv_flood.from_slow, kv_flood.from_mid, kv_flood.from_last):
        step(0, lambda src, u: None)
    for k in range(1, E):
        src = lax.rem(me + k, E)
        exchange(q_all, q_send, q_recv, k, src).wait_recv()
        exchange(meta_all, m_send, m_recv, k, src).wait_recv()

    @pl.loop(0, E)
    def _(i):
        b = lax.rem(me + 1 + i, E)
        meta = meta_all[b]
        local = meta[0:1, :] - (me * per_dev).astype(F32)
        inside_row = (local >= 0.0) & (local < per_dev)
        local_col = to_column(local)
        gate_col = to_column(meta[4:5, :])
        inside_col = (local_col >= 0.0) & (local_col < per_dev)
        q = q_all[b]
        scores = jnp.zeros((rows, keys), F32)
        of_head = [
            (local_col >= h * group) & (local_col < (h + 1) * group) for h in range(heads)
        ]
        for h in range(heads):
            k_h = kv_all[:, 0, :, h * hd : (h + 1) * hd].reshape(keys, hd)
            s_h = lax.dot_general(q, k_h, (((1,), (1,)), ((), ())), preferred_element_type=F32)
            scores = jnp.where(of_head[h], s_h, scores)
        scores = scores * hd ** (-0.5)
        first = (b * n + ctx) * tok_dev
        visible = iota((rows, keys), 1) <= first + iota((rows, keys), 0) // top
        scores = jnp.where(visible, scores, -1e30)
        peak = jnp.max(scores, axis=1, keepdims=True)
        weights = jnp.where(visible, jnp.exp(scores - peak), 0.0)
        total = jnp.sum(weights, axis=1, keepdims=True)
        mixed = jnp.zeros((rows, hd), F32)
        for h in range(heads):
            v_h = kv_all[:, 0, :, (heads + h) * hd : (heads + h + 1) * hd].reshape(keys, hd)
            mixed += jnp.dot(
                jnp.where(of_head[h], weights, 0.0).astype(BF16), v_h, preferred_element_type=F32
            )
        gated = (gate_col * (mixed / total)).astype(BF16)
        before = (iota((rows, rows), 0) < iota((rows, rows), 1)) & inside_col
        rank_row = jnp.sum(jnp.where(before, 1.0, 0.0), axis=0, keepdims=True)
        slot_row = jnp.where(inside_row, rank_row, -1.0)
        slot_col = to_column(slot_row)
        pick = (iota((slots, rows), 0).astype(F32) == slot_row).astype(F32).astype(BF16)
        packed = jnp.dot(pick, gated, preferred_element_type=F32).astype(BF16)
        place = local_col * tok_dev + (iota((rows, 1), 0) // top).astype(F32)
        placed = slot_col == iota((rows, LANES), 1).astype(F32)
        target = jnp.sum(jnp.where(placed, place + 1.0, 0.0), axis=0, keepdims=True) - 1.0
        g_all[ctx, b, 0:slots, :] = packed
        g_all[ctx, b, slots : slots + META_ROWS, :] = jnp.broadcast_to(
            target, (META_ROWS, LANES)
        ).astype(BF16)
        g_flood.begin(b)

    def expand(src, b):
        shard = g_all[src, b]
        target = shard[slots:, :].astype(F32)[0:1, : slots + META_ROWS]
        where = (
            iota((per_dev * tok_dev, slots + META_ROWS), 0).astype(F32) == target
        ).astype(F32).astype(BF16)
        spread = jnp.dot(where, shard, preferred_element_type=F32)
        at = pl.ds(pl.multiple_of((b * n + src) * tok_dev, tok_dev), tok_dev)
        for x in range(per_dev):
            dense[at, x * hd : (x + 1) * hd] = spread[x * tok_dev : (x + 1) * tok_dev, :]

    half = n * tok_dev
    depth = per_dev * hd
    chunk = min(512, depth)
    parts, width = part_in.shape[1], part_in.shape[3]

    def project(b, p):
        acc[...] = jnp.zeros_like(acc)
        base = pl.multiple_of(b * half, half)

        @pl.loop(0, depth // chunk)
        def _(j):
            at = pl.ds(pl.multiple_of(j * chunk, chunk), chunk)
            acc[...] += jnp.dot(
                dense[pl.ds(base, half), at].astype(BF16),
                w_all[at, p * width : (p + 1) * width],
                preferred_element_type=F32,
            )
        return acc[...].astype(BF16)

    def send_part(k, p):
        return pltpu.make_async_remote_copy(
            src_ref=part_out.at[k, p],
            dst_ref=part_in.at[E - k, p],
            send_sem=p_send.at[k, p],
            recv_sem=p_recv.at[E - k, p],
            device_id={"exp": lax.rem(me + k, E)},
            device_id_type=MESH,
        )

    w_copy.wait()
    halves = [lax.rem(me + 1 + i, E) for i in range(E)]

    def finish(i):
        k = (i + 1) % E
        for p in range(parts):
            part_out[k, p] = project(halves[i], p)
            if k:
                send_part(k, p).start()

    for i in range(E):
        g_flood.from_slow(halves[i], expand)
        if i:
            g_flood.from_last(halves[i - 1], expand)
            expand(ctx, halves[i - 1])
            finish(i - 1)
        g_flood.from_mid(halves[i], expand)
    g_flood.from_last(me, expand)
    expand(ctx, me)
    finish(E - 1)
    kv_flood.end()
    g_flood.end()
    for k in range(1, E):
        exchange(q_all, q_send, q_recv, k, me).wait_send()
        exchange(meta_all, m_send, m_recv, k, me).wait_send()
    for p in range(parts):
        total = part_out[0, p].astype(F32)
        for k in range(1, E):
            send_part(E - k, p).wait_recv()
            total += part_in[k, p].astype(F32)
        out_ref[:, p * width : (p + 1) * width] = total.astype(BF16)
    for k in range(1, E):
        for p in range(parts):
            send_part(k, p).wait_send()


def body(queries, key_heads, value_heads, expert_ids, gate_logits, out_weight):
    n = lax.axis_size("ctx")
    E = lax.axis_size("exp")
    tok_dev, top, hd = queries.shape
    rows = tok_dev * top
    span, heads, _ = key_heads.shape
    per_dev, _, cols = out_weight.shape
    slots = -(-per_dev * MOST // 16) * 16
    parts = max(1, cols // 256)
    vmem = pl.BlockSpec(memory_space=pltpu.VMEM)
    dma = pltpu.SemaphoreType.DMA
    return pl.pallas_call(
        functools.partial(kernel, n, E, top),
        out_shape=jax.ShapeDtypeStruct((n * tok_dev, cols), BF16),
        in_specs=[pl.BlockSpec(memory_space=pltpu.HBM)] * 6,
        out_specs=vmem,
        scratch_shapes=[
            pltpu.VMEM((span, heads, hd), BF16),
            pltpu.VMEM((span, heads, hd), BF16),
            pltpu.VMEM((tok_dev, top), jnp.int32),
            pltpu.VMEM((tok_dev, top), F32),
            pltpu.VMEM((E, rows, hd), BF16),
            pltpu.VMEM((E, 8, rows), F32),
            pltpu.VMEM((n, 1, span, 2 * heads * hd), BF16),
            pltpu.VMEM((n, E, slots + META_ROWS, hd), BF16),
            pltpu.VMEM((E * n * tok_dev, per_dev * hd), F32),
            pltpu.VMEM((per_dev * hd, cols), BF16),
            pltpu.VMEM((E, parts, n * tok_dev, cols // parts), BF16),
            pltpu.VMEM((E, parts, n * tok_dev, cols // parts), BF16),
            pltpu.VMEM((n * tok_dev, cols // parts), F32),
            dma((3, n, 1)), dma((n, 1)), dma((3, n, E)), dma((n, E)),
            dma((E,)), dma((E,)), dma((E,)), dma((E,)), dma((E, parts)), dma((E, parts)),
            dma, dma((5,)),
        ],
        compiler_params=pltpu.CompilerParams(
            collective_id=0, has_side_effects=True, vmem_limit_bytes=54 * 2**20
        ),
    )(queries.reshape(rows, hd), key_heads, value_heads, expert_ids, gate_logits, out_weight.reshape(per_dev * hd, cols))


def solution(mesh):
    in_specs = (
        P(("exp", "ctx"), None, None),
        P("ctx", "exp", None),
        P("ctx", "exp", None),
        P(("exp", "ctx"), None),
        P(("exp", "ctx"), None),
        P("exp", None, "ctx"),
    )
    out_specs = P("exp", "ctx")
    return jax.shard_map(body, mesh=mesh, in_specs=in_specs, out_specs=out_specs, check_vma=False)
```
